32 devices in a mesh: parts: 2 (over y), seq: 4 (over z), dp: 2 (over x), fsdp: 2 (over core).
Axes of the slice: x: 2, y: 2, z: 4, core: 2. Of those that a mesh axis runs over, the one named last changes fastest.
Arguments:
- queries: bfloat16 [8, 512, 2048], P(('parts', 'dp', 'fsdp'), 'seq'), parts along dimension 0, may hold values from -6 to 6
- key_states: bfloat16 [8, 512, 512], P(('parts', 'dp', 'fsdp'), 'seq'), parts along dimension 0, may hold values from -6 to 6
- values: bfloat16 [8, 512, 512], P(('parts', 'dp', 'fsdp'), 'seq'), parts along dimension 0, may hold values from -6 to 6
- grad_out: bfloat16 [8, 512, 2048], P(('parts', 'dp', 'fsdp'), 'seq'), parts along dimension 0, may hold values from -6 to 6
- segments: int32 [8, 512], P(('parts', 'dp', 'fsdp'), 'seq'), parts along dimension 0, may hold values from 0 to 7, never falling along the last dimension, each value on 1 to 256 neighbouring positions
Outputs:
- attended: bfloat16 [8, 512, 2048], P(('parts', 'dp', 'fsdp'), 'seq'), parts along dimension 0
- query_grad: bfloat16 [8, 512, 2048], P(('parts', 'dp', 'fsdp'), 'seq'), parts along dimension 0
- key_grad: bfloat16 [8, 512, 512], P(('parts', 'dp', 'fsdp'), 'seq'), parts along dimension 0
- value_grad: bfloat16 [8, 512, 512], P(('parts', 'dp', 'fsdp'), 'seq'), parts along dimension 0
The draws below stay inside these ranges and needn't reach their ends.
There are 2 independent parts, one for each index of `parts`. The reference program is written for one: setup_inputs(seed, part) draws one part's arguments, and reference() takes and returns one part's arrays. A program takes and returns all parts, laid end to end along the dimension named above; each array names one. Nothing has to cross between parts.
Inputs may be any that keep to these rules, and one draw needn't show every extreme that they name: `segments`: document numbers never fall along a row; every document has 1 to 256 tokens and one of each row has exactly 256.
All inputs are finite; a program needn't handle non-finite values.
Results may differ from the reference program's by a relative error of at most 0.0093.
Values may be sent and summed in bfloat16 or wider, within the bound.
A program may use at most 64 MiB of HBM per device.

```python
import math
import jax
import jax.numpy as jnp
import numpy as np
from jax import lax

H = 16
KVH = 4
HD = 128
DOCS = 8
SEQLEN = 512
BATCH = 4
MOST = 256
N_SEQ = 4


def draw_queries(key, part):
    key = jax.random.fold_in(key, 11)
    drawn = jax.random.truncated_normal(key, -5.5, 5.5, (BATCH, SEQLEN, H, HD), jnp.float32)
    return drawn.reshape(BATCH, SEQLEN, H * HD).astype(jnp.bfloat16)


def draw_key_states(key, part):
    key = jax.random.fold_in(key, 23)
    drawn = jax.random.truncated_normal(key, -5.5, 5.5, (BATCH, SEQLEN, KVH, HD), jnp.float32)
    return drawn.reshape(BATCH, SEQLEN, KVH * HD).astype(jnp.bfloat16)


def block_levels(rng, dims, split, least, largest):
    def one(dim, shards_of):
        draws = jax.random.uniform(jax.random.fold_in(jax.random.fold_in(rng, 6), dim), (shards_of,), jnp.float32, least / len(split), largest / len(split))
        return jnp.repeat(jnp.exp(draws), dims[dim] // shards_of).reshape((-1,) + (1,) * (len(dims) - dim - 1))

    gain = one(*split[0])
    for cut in split[1:]:
        gain = gain * one(*cut)
    return gain


def split_up(count, total, most, skew):
    weights = [(1 << 20) // math.isqrt(standing ** skew) + 1 for standing in range(2, count + 1)]
    rest, holding = total - most - (count - 1), [1] * (count - 1)
    while rest > 0:
        movable = [i for i in range(count - 1) if holding[i] < most]
        whole, budget = sum([weights[i] for i in movable]), rest
        for i in movable:
            addition = min(most - holding[i], max(1, budget * weights[i] // whole), rest)
            holding[i] = holding[i] + addition
            rest = rest - addition
    return np.array([most] + holding)


def uneven_parts(stream_key, number_of, total, most, slope):
    if number_of == 2:
        one = jax.random.randint(stream_key, (), max(1, total - most), min(most, total - 1) + 1)
        return jnp.stack([one, total - one])
    lengths = jnp.asarray(split_up(number_of, total, most, slope), jnp.int32)
    couples = (number_of - 1) // 2
    giver, sink = lengths[1:1 + 2 * couples:2], lengths[2:2 + 2 * couples:2]
    room = jnp.minimum(giver - 1, most - sink)
    shifted = jax.random.randint(jax.random.fold_in(stream_key, 1), (couples,), 0, 1 << 20) % (room + 1)
    lengths = lengths.at[1:1 + 2 * couples:2].set(giver - shifted).at[2:2 + 2 * couples:2].set(sink + shifted)
    return lengths[jax.random.permutation(jax.random.fold_in(stream_key, 2), number_of)]


def noise(stream_key, shape, scale, bound, shards=(), held_as=jnp.bfloat16):
    array = scale * jax.random.normal(stream_key, shape, jnp.float32)
    if shards:
        array = array * block_levels(stream_key, shape, shards, -0.22, 0.18)
    return jnp.clip(array, -bound, bound).astype(held_as)


def setup_inputs(seed: int = 0, part: int = 0) -> dict:
    arg_keys = jax.random.split(jax.random.key(seed), 6)
    own_keys = jax.random.split(jax.random.fold_in(arg_keys[5], part), 6)
    return {
        "queries": draw_queries(jax.random.fold_in(jax.random.fold_in(arg_keys[5], part), 71), part),
        "key_states": draw_key_states(jax.random.fold_in(jax.random.fold_in(arg_keys[5], part), 71), part),
        "values": noise(own_keys[2], (BATCH, SEQLEN, KVH * HD), 1.0, 6.0, ((0, 4), (1, 4))),
        "grad_out": noise(own_keys[3], (BATCH, SEQLEN, H * HD), 1.0, 6.0, ((0, 4), (1, 4))),
        "segments": jax.vmap(lambda own: jnp.searchsorted(jnp.cumsum(uneven_parts(own, DOCS, SEQLEN, MOST, 2)), jnp.arange(SEQLEN), side="right"))(jax.random.split(own_keys[4], BATCH)).reshape((BATCH, SEQLEN)).astype(jnp.int32),
    }


def one_head(inputs):
    query_head, key_head, value_head, grad_head, segment_ids = inputs
    score_scale = HD ** -0.5
    positions = jnp.arange(SEQLEN, dtype=jnp.int32)
    allowed = (positions[:, None] >= positions[None, :]) & (segment_ids[:, None] == segment_ids[None, :])
    scores = jnp.dot(query_head, key_head.T, preferred_element_type=jnp.float32) * score_scale
    masked = jnp.where(allowed, scores, -jnp.inf)
    row_max = jnp.max(masked, axis=1, keepdims=True)
    exponents = jnp.where(allowed, jnp.exp(masked - row_max), 0.0)
    weights = exponents / jnp.sum(exponents, axis=1, keepdims=True)
    weights_low = weights.astype(jnp.bfloat16)
    attended = jnp.dot(weights_low, value_head, preferred_element_type=jnp.float32)
    spread = jnp.dot(grad_head, value_head.T, preferred_element_type=jnp.float32)
    row_delta = jnp.sum(grad_head.astype(jnp.float32) * attended, axis=1, keepdims=True)
    score_grad = (weights * (spread - row_delta)).astype(jnp.bfloat16)
    query_grad = jnp.dot(score_grad, key_head, preferred_element_type=jnp.float32) * score_scale
    key_grad = jnp.dot(score_grad.T, query_head, preferred_element_type=jnp.float32) * score_scale
    value_grad = jnp.dot(weights_low.T, grad_head, preferred_element_type=jnp.float32)
    return attended, query_grad, key_grad, value_grad


def split_heads(array_in, head_count):
    return array_in.reshape(BATCH, SEQLEN, head_count, HD).transpose(0, 2, 1, 3).reshape(BATCH * head_count, SEQLEN, HD)


def merge_heads(array_in, head_count):
    return array_in.reshape(BATCH, head_count, SEQLEN, HD).transpose(0, 2, 1, 3).reshape(BATCH, SEQLEN, head_count * HD).astype(jnp.bfloat16)


def group_sum(array_in, group_ratio):
    copies = max(1, N_SEQ // KVH)
    per_group = group_ratio // copies
    parts_low = array_in.reshape(BATCH, KVH, copies, per_group, SEQLEN, HD).sum(axis=3).astype(jnp.bfloat16)
    return parts_low.astype(jnp.float32).sum(axis=2).reshape(BATCH * KVH, SEQLEN, HD)


def reference(queries, key_states, values, grad_out, segments):
    group_ratio = H // KVH
    key_heads = jnp.repeat(key_states.reshape(BATCH, SEQLEN, KVH, HD), group_ratio, axis=2)
    value_heads = jnp.repeat(values.reshape(BATCH, SEQLEN, KVH, HD), group_ratio, axis=2)
    inputs = (split_heads(queries, H), split_heads(key_heads, H), split_heads(value_heads, H), split_heads(grad_out, H), jnp.repeat(segments, H, axis=0))
    attended, query_grad, key_grad, value_grad = lax.map(one_head, inputs)
    key_grad = group_sum(key_grad, group_ratio)
    value_grad = group_sum(value_grad, group_ratio)
    return merge_heads(attended, H), merge_heads(query_grad, H), merge_heads(key_grad, KVH), merge_heads(value_grad, KVH)
```

```python
import functools

import jax
import jax.numpy as jnp
from jax import lax
from jax.experimental import pallas as pl
from jax.experimental.pallas import tpu as pltpu
from jax.sharding import PartitionSpec as P

H = 16
KVH = 4
HD = 128
RATIO = H // KVH
PAIR = 2
masked_bias = -1e30
MESH = pl.DeviceIdType.MESH


def kernel(
    members,
    reach,
    q_hbm,
    k_hbm,
    v_hbm,
    g_hbm,
    s_hbm,
    o_hbm,
    dq_hbm,
    dk_hbm,
    dv_hbm,
    q_buf,
    g_buf,
    kv_buf,
    o_buf,
    dq_buf,
    own,
    outgoing,
    incoming,
    dkv_buf,
    seg_row,
    seg_buf,
    bias,
    in_sem,
    out_sem,
    seg_sem,
    seg_send,
    seg_recv,
    kv_send,
    kv_recv,
    part_send,
    part_recv,
):
    me = lax.axis_index("seq")
    rows = q_buf.shape[1]
    keys = (reach + 1) * rows
    scale = HD**-0.5
    has_left = me > 0
    has_right = me < members - 1

    def columns(g, width):
        return pl.ds(pl.multiple_of(g * width, width), width)

    def loads(g):
        return (
            pltpu.make_async_copy(k_hbm.at[0, :, columns(g, HD)], kv_buf.at[0, g, 0], in_sem.at[0, g]),
            pltpu.make_async_copy(v_hbm.at[0, :, columns(g, HD)], kv_buf.at[0, g, 1], in_sem.at[1, g]),
            pltpu.make_async_copy(q_hbm.at[0, :, columns(g, RATIO * HD)], q_buf.at[g], in_sem.at[2, g]),
            pltpu.make_async_copy(g_hbm.at[0, :, columns(g, RATIO * HD)], g_buf.at[g], in_sem.at[3, g]),
        )

    def stores(g):
        return (
            pltpu.make_async_copy(o_buf.at[g], o_hbm.at[0, :, columns(g, RATIO * HD)], out_sem.at[0, g]),
            pltpu.make_async_copy(dq_buf.at[g], dq_hbm.at[0, :, columns(g, RATIO * HD)], out_sem.at[1, g]),
            pltpu.make_async_copy(dkv_buf.at[g, 0], dk_hbm.at[0, :, columns(g, HD)], out_sem.at[2, g]),
            pltpu.make_async_copy(dkv_buf.at[g, 1], dv_hbm.at[0, :, columns(g, HD)], out_sem.at[3, g]),
        )

    def kv_copy(w, g):
        return pltpu.make_async_remote_copy(
            src_ref=kv_buf.at[w, g],
            dst_ref=kv_buf.at[w + 1, g],
            send_sem=kv_send.at[w, g],
            recv_sem=kv_recv.at[w, g],
            device_id={"seq": lax.rem(me + 1, members)},
            device_id_type=MESH,
        )

    def seg_copy(w):
        return pltpu.make_async_remote_copy(
            src_ref=seg_buf.at[w],
            dst_ref=seg_buf.at[w + 1],
            send_sem=seg_send.at[w],
            recv_sem=seg_recv.at[w],
            device_id={"seq": lax.rem(me + 1, members)},
            device_id_type=MESH,
        )

    def part_copy(s, g):
        return pltpu.make_async_remote_copy(
            src_ref=outgoing.at[s, g],
            dst_ref=incoming.at[s, g],
            send_sem=part_send.at[s, g],
            recv_sem=part_recv.at[s, g],
            device_id={"seq": lax.rem(me + members - 1, members)},
            device_id_type=MESH,
        )

    seg_load = pltpu.make_async_copy(s_hbm, seg_row, seg_sem)
    seg_load.start()
    for g in range(KVH):
        for copy in loads(g)[:2]:
            copy.start()
    for g in range(KVH):
        for copy in loads(g)[2:]:
            copy.start()

    barrier = pltpu.get_barrier_semaphore()

    @pl.when(has_left)
    def _():
        pl.semaphore_signal(
            barrier, inc=1, device_id={"seq": lax.rem(me + members - 1, members)}, device_id_type=MESH
        )

    @pl.when(has_right)
    def _():
        pl.semaphore_signal(
            barrier, inc=1, device_id={"seq": lax.rem(me + 1, members)}, device_id_type=MESH
        )

    for w in range(1, reach + 1):

        @pl.when(me < w)
        def _(w=w):
            kv_buf[w] = jnp.zeros(kv_buf.shape[1:], kv_buf.dtype)
            seg_buf[w] = jnp.zeros(seg_buf.shape[1:], seg_buf.dtype)

    seg_load.wait()
    seg_buf[0] = jnp.broadcast_to(seg_row[...], seg_buf.shape[1:])
    neighbours = has_left.astype(jnp.int32) + has_right.astype(jnp.int32)
    pl.semaphore_wait(barrier, neighbours)

    def send_own(g):
        for copy in loads(g)[:2]:
            copy.wait()

        @pl.when(has_right)
        def _():
            kv_copy(0, g).start()

    def forward(g):
        for w in range(1, reach):

            @pl.when(me >= w)
            def _(w=w):
                kv_copy(w - 1, g).wait_recv()

                @pl.when(has_right)
                def _():
                    kv_copy(w, g).start()

    @pl.when(has_right)
    def _():
        seg_copy(0).start()

    send_own(0)
    send_own(1)
    for w in range(1, reach + 1):

        @pl.when(me >= w)
        def _(w=w):
            seg_copy(w - 1).wait_recv()
            if w < reach:

                @pl.when(has_right)
                def _():
                    seg_copy(w).start()

    forward(0)

    row_ids = lax.broadcasted_iota(jnp.int32, (rows, rows), 0)
    column_ids = lax.broadcasted_iota(jnp.int32, (rows, rows), 1)
    own_document = jnp.broadcast_to(seg_buf[0, 0:1].astype(jnp.float32), (rows, rows))
    for w in range(reach + 1):
        key_document = jnp.broadcast_to(seg_buf[w, 0:1].astype(jnp.float32), (rows, rows)).T
        allowed = key_document == own_document
        if w == 0:
            allowed = jnp.logical_and(allowed, row_ids <= column_ids)
        block = jnp.where(allowed, 0.0, masked_bias)
        bias[pl.ds(w * rows, rows)] = jnp.where(me >= w, block, masked_bias)

    def contract(left, right):
        return lax.dot_general(left, right, (((1,), (1,)), ((), ())), preferred_element_type=jnp.float32)

    def product(left, right):
        return jnp.dot(left, right, preferred_element_type=jnp.float32)

    def compute(g):
        key = kv_buf[:, g, 0].reshape(keys, HD)
        value = kv_buf[:, g, 1].reshape(keys, HD)
        key_t = key.T
        value_t = value.T
        shift = jnp.concatenate([bias[...]] * PAIR, axis=1)
        key_sum = value_sum = None
        for first in range(0, RATIO, PAIR):
            heads = range(first, first + PAIR)
            query = jnp.concatenate([q_buf[g, :, h * HD : (h + 1) * HD] for h in heads], axis=0)
            grad = jnp.concatenate([g_buf[g, :, h * HD : (h + 1) * HD] for h in heads], axis=0)
            scores = contract(key, query) * scale + shift
            top = jnp.max(scores, axis=0, keepdims=True)
            exponents = jnp.exp(scores - top)
            weights = exponents * (1.0 / jnp.sum(exponents, axis=0, keepdims=True))
            weights_low = weights.astype(jnp.bfloat16)
            spread = contract(value, grad)
            delta = jnp.sum(weights_low.astype(jnp.float32) * spread, axis=0, keepdims=True)
            score_grad = (weights * (spread - delta)).astype(jnp.bfloat16)
            attended = product(value_t, weights_low).T.astype(jnp.bfloat16)
            query_grad = (product(key_t, score_grad) * scale).T.astype(jnp.bfloat16)
            for at, h in enumerate(heads):
                o_buf[g, :, h * HD : (h + 1) * HD] = attended[at * rows : (at + 1) * rows]
                dq_buf[g, :, h * HD : (h + 1) * HD] = query_grad[at * rows : (at + 1) * rows]
            key_part = product(score_grad, query)
            value_part = product(weights_low, grad)
            key_sum = key_part if key_sum is None else key_sum + key_part
            value_sum = value_part if value_sum is None else value_sum + value_part
        key_sum = key_sum * scale
        for w in range(reach + 1):
            block = slice(w * rows, (w + 1) * rows)
            if w < reach:
                own[g, w, 0] = key_sum[block]
                own[g, w, 1] = value_sum[block]
            else:
                outgoing[w - 1, g, 0] = key_sum[block].astype(jnp.bfloat16)
                outgoing[w - 1, g, 1] = value_sum[block].astype(jnp.bfloat16)

    def pass_on(g):
        for w in range(reach - 1, 0, -1):

            @pl.when(me >= w)
            def _(w=w):
                @pl.when(has_right)
                def _():
                    part_copy(w, g).wait_recv()
                    outgoing[w - 1, g] = (own[g, w] + incoming[w, g].astype(jnp.float32)).astype(jnp.bfloat16)

                @pl.when(jnp.logical_not(has_right))
                def _():
                    outgoing[w - 1, g] = own[g, w].astype(jnp.bfloat16)

                part_copy(w - 1, g).start()

    def finish(g):
        @pl.when(has_right)
        def _():
            part_copy(0, g).wait_recv()
            dkv_buf[g] = (own[g, 0] + incoming[0, g].astype(jnp.float32)).astype(jnp.bfloat16)

        @pl.when(jnp.logical_not(has_right))
        def _():
            dkv_buf[g] = own[g, 0].astype(jnp.bfloat16)

        for copy in stores(g)[2:]:
            copy.start()

    def step(g, carry):
        @pl.when(g + 2 < KVH)
        def _():
            send_own(g + 2)

        @pl.when(g + 1 < KVH)
        def _():
            forward(g + 1)

        @pl.when(me >= reach)
        def _():
            kv_copy(reach - 1, g).wait_recv()

        for copy in loads(g)[2:]:
            copy.wait()
        compute(g)

        @pl.when(me >= reach)
        def _():
            part_copy(reach - 1, g).start()

        for copy in stores(g)[:2]:
            copy.start()

        @pl.when(g >= 1)
        def _():
            pass_on(g - 1)

        return carry

    lax.fori_loop(0, KVH, step, 0)
    pass_on(KVH - 1)
    for g in range(KVH):
        finish(g)

    for w in range(reach):

        @pl.when(jnp.logical_and(has_right, me >= w))
        def _(w=w):
            seg_copy(w).wait_send()
            for g in range(KVH):
                kv_copy(w, g).wait_send()

        @pl.when(me >= w + 1)
        def _(w=w):
            for g in range(KVH):
                part_copy(w, g).wait_send()

    for g in range(KVH):
        for copy in stores(g):
            copy.wait()


def local(members, queries, key_states, values, grad_out, segments):
    rows = queries.shape[1]
    reach = max(1, members // 2)
    any_space = pl.BlockSpec(memory_space=pl.ANY)
    low = jnp.bfloat16
    dma = pltpu.SemaphoreType.DMA
    pairs = H * rows * (reach + 1) * rows
    return pl.pallas_call(
        functools.partial(kernel, members, reach),
        out_shape=(
            jax.ShapeDtypeStruct(queries.shape, low),
            jax.ShapeDtypeStruct(queries.shape, low),
            jax.ShapeDtypeStruct(key_states.shape, low),
            jax.ShapeDtypeStruct(values.shape, low),
        ),
        in_specs=[any_space] * 5,
        out_specs=(any_space,) * 4,
        scratch_shapes=[
            pltpu.VMEM((KVH, rows, RATIO * HD), low),
            pltpu.VMEM((KVH, rows, RATIO * HD), low),
            pltpu.VMEM((reach + 1, KVH, 2, rows, HD), low),
            pltpu.VMEM((KVH, rows, RATIO * HD), low),
            pltpu.VMEM((KVH, rows, RATIO * HD), low),
            pltpu.VMEM((KVH, reach, 2, rows, HD), jnp.float32),
            pltpu.VMEM((reach, KVH, 2, rows, HD), low),
            pltpu.VMEM((reach, KVH, 2, rows, HD), low),
            pltpu.VMEM((KVH, 2, rows, HD), low),
            pltpu.VMEM((1, rows), jnp.int32),
            pltpu.VMEM((reach + 1, 8, rows), jnp.int32),
            pltpu.VMEM(((reach + 1) * rows, rows), jnp.float32),
            dma((4, KVH)),
            dma((4, KVH)),
            dma,
            dma((reach,)),
            dma((reach,)),
            dma((reach, KVH)),
            dma((reach, KVH)),
            dma((reach, KVH)),
            dma((reach, KVH)),
        ],
        compiler_params=pltpu.CompilerParams(
            collective_id=0, has_side_effects=True, vmem_limit_bytes=40 * 1024 * 1024
        ),
        cost_estimate=pl.CostEstimate(
            flops=12 * pairs * HD, bytes_accessed=4 * queries.size * 2 + 8 * values.size * 2, transcendentals=pairs
        ),
    )(queries, key_states, values, grad_out, segments)


def solution(mesh):
    spread = ("parts", "dp", "fsdp")
    wide = P(spread, "seq", None)
    return jax.shard_map(
        functools.partial(local, mesh.shape["seq"]),
        mesh=mesh,
        in_specs=(wide, wide, wide, wide, P(spread, "seq")),
        out_specs=(wide, wide, wide, wide),
        check_vma=False,
    )
```

```python
import functools

import jax
import jax.numpy as jnp
from jax import lax
from jax.experimental import pallas as pl
from jax.experimental.pallas import tpu as pltpu
from jax.sharding import PartitionSpec as P

H = 16
KVH = 4
HD = 128
RATIO = H // KVH
PAIR = 2
masked_bias = -1e30
MESH = pl.DeviceIdType.MESH


def kernel(
    members,
    reach,
    q_hbm,
    k_hbm,
    v_hbm,
    g_hbm,
    s_hbm,
    o_hbm,
    dq_hbm,
    dk_hbm,
    dv_hbm,
    q_buf,
    g_buf,
    kv_buf,
    o_buf,
    dq_buf,
    own,
    outgoing,
    incoming,
    dkv_buf,
    seg_row,
    seg_buf,
    bias,
    in_sem,
    out_sem,
    seg_sem,
    seg_send,
    seg_recv,
    kv_send,
    kv_recv,
    part_send,
    part_recv,
):
    me = lax.axis_index("seq")
    rows = q_buf.shape[1]
    keys = (reach + 1) * rows
    scale = HD**-0.5
    has_left = me > 0
    has_right = me < members - 1

    def columns(g, width):
        return pl.ds(pl.multiple_of(g * width, width), width)

    def kv_loads(g):
        return (
            pltpu.make_async_copy(k_hbm.at[0, :, columns(g, HD)], kv_buf.at[0, g, 0], in_sem.at[0, g]),
            pltpu.make_async_copy(v_hbm.at[0, :, columns(g, HD)], kv_buf.at[0, g, 1], in_sem.at[1, g]),
        )

    def loads(g):
        return (
            pltpu.make_async_copy(q_hbm.at[0, :, columns(g, RATIO * HD)], q_buf.at[g], in_sem.at[2, g]),
            pltpu.make_async_copy(g_hbm.at[0, :, columns(g, RATIO * HD)], g_buf.at[g], in_sem.at[3, g]),
        )

    def stores(g):
        return (
            pltpu.make_async_copy(o_buf.at[g], o_hbm.at[0, :, columns(g, RATIO * HD)], out_sem.at[0, g]),
            pltpu.make_async_copy(dq_buf.at[g], dq_hbm.at[0, :, columns(g, RATIO * HD)], out_sem.at[1, g]),
        )

    def kv_stores(g):
        return (
            pltpu.make_async_copy(dkv_buf.at[g, 0], dk_hbm.at[0, :, columns(g, HD)], out_sem.at[2, g]),
            pltpu.make_async_copy(dkv_buf.at[g, 1], dv_hbm.at[0, :, columns(g, HD)], out_sem.at[3, g]),
        )

    def kv_copy(w, g, t):
        return pltpu.make_async_remote_copy(
            src_ref=kv_buf.at[w, g, t],
            dst_ref=kv_buf.at[w + 1, g, t],
            send_sem=kv_send.at[w, g, t],
            recv_sem=kv_recv.at[w, g, t],
            device_id={"seq": lax.rem(me + 1, members)},
            device_id_type=MESH,
        )

    def seg_copy(w):
        return pltpu.make_async_remote_copy(
            src_ref=seg_buf.at[w],
            dst_ref=seg_buf.at[w + 1],
            send_sem=seg_send.at[w],
            recv_sem=seg_recv.at[w],
            device_id={"seq": lax.rem(me + 1, members)},
            device_id_type=MESH,
        )

    def part_copy(s, g, t):
        return pltpu.make_async_remote_copy(
            src_ref=outgoing.at[s, g, t],
            dst_ref=incoming.at[s, g, t],
            send_sem=part_send.at[s, g, t],
            recv_sem=part_recv.at[s, g, t],
            device_id={"seq": lax.rem(me + members - 1, members)},
            device_id_type=MESH,
        )

    seg_load = pltpu.make_async_copy(s_hbm, seg_row, seg_sem)
    seg_load.start()
    for g in range(KVH):
        for copy in kv_loads(g):
            copy.start()
    for g in range(KVH):
        for copy in loads(g):
            copy.start()

    barrier = pltpu.get_barrier_semaphore()

    @pl.when(has_left)
    def _():
        pl.semaphore_signal(
            barrier, inc=1, device_id={"seq": lax.rem(me + members - 1, members)}, device_id_type=MESH
        )

    @pl.when(has_right)
    def _():
        pl.semaphore_signal(
            barrier, inc=1, device_id={"seq": lax.rem(me + 1, members)}, device_id_type=MESH
        )

    for w in range(1, reach + 1):

        @pl.when(me < w)
        def _(w=w):
            kv_buf[w] = jnp.zeros(kv_buf.shape[1:], kv_buf.dtype)
            seg_buf[w] = jnp.zeros(seg_buf.shape[1:], seg_buf.dtype)

    seg_load.wait()
    seg_buf[0] = jnp.broadcast_to(seg_row[...], seg_buf.shape[1:])
    neighbours = has_left.astype(jnp.int32) + has_right.astype(jnp.int32)
    pl.semaphore_wait(barrier, neighbours)

    def send_own(g):
        for copy in kv_loads(g):
            copy.wait()

        @pl.when(has_right)
        def _():
            kv_copy(0, g, 0).start()
            kv_copy(0, g, 1).start()

    def forward(g):
        for w in range(1, reach):

            @pl.when(me >= w)
            def _(w=w):
                for t in range(2):
                    kv_copy(w - 1, g, t).wait_recv()

                    @pl.when(has_right)
                    def _(t=t):
                        kv_copy(w, g, t).start()

    @pl.when(has_right)
    def _():
        seg_copy(0).start()

    send_own(0)
    send_own(1)
    forward(0)
    for w in range(1, reach + 1):

        @pl.when(me >= w)
        def _(w=w):
            seg_copy(w - 1).wait_recv()
            if w < reach:

                @pl.when(has_right)
                def _():
                    seg_copy(w).start()

    row_ids = lax.broadcasted_iota(jnp.int32, (rows, rows), 0)
    column_ids = lax.broadcasted_iota(jnp.int32, (rows, rows), 1)
    own_document = jnp.broadcast_to(seg_buf[0, 0:1].astype(jnp.float32), (rows, rows))
    for w in range(reach + 1):
        key_document = jnp.broadcast_to(seg_buf[w, 0:1].astype(jnp.float32), (rows, rows)).T
        allowed = key_document == own_document
        if w == 0:
            allowed = jnp.logical_and(allowed, row_ids <= column_ids)
        block = jnp.where(allowed, 0.0, masked_bias)
        bias[pl.ds(w * rows, rows)] = jnp.where(me >= w, block, masked_bias)

    def contract(left, right):
        return lax.dot_general(left, right, (((1,), (1,)), ((), ())), preferred_element_type=jnp.float32)

    def product(left, right):
        return jnp.dot(left, right, preferred_element_type=jnp.float32)

    def compute(g):
        key = kv_buf[:, g, 0].reshape(keys, HD)
        value = kv_buf[:, g, 1].reshape(keys, HD)
        key_t = key.T
        value_t = value.T
        shift = jnp.concatenate([bias[...]] * PAIR, axis=1)
        key_sum = value_sum = None
        for first in range(0, RATIO, PAIR):
            heads = range(first, first + PAIR)
            query = jnp.concatenate([q_buf[g, :, h * HD : (h + 1) * HD] for h in heads], axis=0)
            grad = jnp.concatenate([g_buf[g, :, h * HD : (h + 1) * HD] for h in heads], axis=0)
            scores = contract(key, query) * scale + shift
            top = jnp.max(scores, axis=0, keepdims=True)
            exponents = jnp.exp(scores - top)
            weights = exponents * (1.0 / jnp.sum(exponents, axis=0, keepdims=True))
            weights_low = weights.astype(jnp.bfloat16)
            spread = contract(value, grad)
            delta = jnp.sum(weights_low.astype(jnp.float32) * spread, axis=0, keepdims=True)
            score_grad = (weights * (spread - delta)).astype(jnp.bfloat16)
            attended = product(value_t, weights_low).T.astype(jnp.bfloat16)
            query_grad = (product(key_t, score_grad) * scale).T.astype(jnp.bfloat16)
            for at, h in enumerate(heads):
                o_buf[g, :, h * HD : (h + 1) * HD] = attended[at * rows : (at + 1) * rows]
                dq_buf[g, :, h * HD : (h + 1) * HD] = query_grad[at * rows : (at + 1) * rows]
            key_part = product(score_grad, query)
            value_part = product(weights_low, grad)
            key_sum = key_part if key_sum is None else key_sum + key_part
            value_sum = value_part if value_sum is None else value_sum + value_part
        key_sum = key_sum * scale
        for w in range(reach + 1):
            block = slice(w * rows, (w + 1) * rows)
            if w < reach:
                own[g, w, 0] = key_sum[block]
                own[g, w, 1] = value_sum[block]
            else:
                outgoing[w - 1, g, 0] = key_sum[block].astype(jnp.bfloat16)
                outgoing[w - 1, g, 1] = value_sum[block].astype(jnp.bfloat16)

    def pass_on(g):
        for w in range(reach - 1, 0, -1):

            @pl.when(me >= w)
            def _(w=w):
                for t in (1, 0):

                    @pl.when(has_right)
                    def _(t=t):
                        part_copy(w, g, t).wait_recv()
                        total = own[g, w, t] + incoming[w, g, t].astype(jnp.float32)
                        outgoing[w - 1, g, t] = total.astype(jnp.bfloat16)

                    @pl.when(jnp.logical_not(has_right))
                    def _(t=t):
                        outgoing[w - 1, g, t] = own[g, w, t].astype(jnp.bfloat16)

                    part_copy(w - 1, g, t).start()

    def finish(g):
        @pl.when(has_right)
        def _():
            part_copy(0, g, 1).wait_recv()
            part_copy(0, g, 0).wait_recv()
            dkv_buf[g] = (own[g, 0] + incoming[0, g].astype(jnp.float32)).astype(jnp.bfloat16)

        @pl.when(jnp.logical_not(has_right))
        def _():
            dkv_buf[g] = own[g, 0].astype(jnp.bfloat16)

        for copy in kv_stores(g):
            copy.start()

    def step(g, carry):
        @pl.when(g + 2 < KVH)
        def _():
            send_own(g + 2)

        @pl.when(g + 1 < KVH)
        def _():
            forward(g + 1)

        @pl.when(me >= reach)
        def _():
            kv_copy(reach - 1, g, 0).wait_recv()
            kv_copy(reach - 1, g, 1).wait_recv()

        for copy in loads(g):
            copy.wait()
        compute(g)

        @pl.when(me >= reach)
        def _():
            part_copy(reach - 1, g, 1).start()
            part_copy(reach - 1, g, 0).start()

        for copy in stores(g):
            copy.start()

        @pl.when(g >= 1)
        def _():
            pass_on(g - 1)

        @pl.when(g >= 2)
        def _():
            finish(g - 2)

        return carry

    lax.fori_loop(0, KVH, step, 0)
    pass_on(KVH - 1)
    finish(KVH - 2)
    finish(KVH - 1)

    for w in range(reach):

        @pl.when(jnp.logical_and(has_right, me >= w))
        def _(w=w):
            seg_copy(w).wait_send()
            for g in range(KVH):
                kv_copy(w, g, 0).wait_send()
                kv_copy(w, g, 1).wait_send()

        @pl.when(me >= w + 1)
        def _(w=w):
            for g in range(KVH):
                part_copy(w, g, 0).wait_send()
                part_copy(w, g, 1).wait_send()

    for g in range(KVH):
        for copy in stores(g) + kv_stores(g):
            copy.wait()


def place(parts, *refs):
    sources, results, held, read_sem, write_sem = refs[0:4], refs[4:8], refs[8:12], refs[12], refs[13]
    pairs = []
    for i in range(4):
        size = sources[i].shape[1] // parts
        for j in range(parts):
            at = (slice(None), pl.ds(j * size, size))
            pairs.append(
                (
                    pltpu.make_async_copy(sources[i].at[at], held[i].at[at], read_sem.at[i, j]),
                    pltpu.make_async_copy(held[i].at[at], results[i].at[at], write_sem.at[i, j]),
                )
            )
    for read, _ in pairs:
        read.start()
    for read, write in pairs:
        read.wait()
        write.start()
    for _, write in pairs:
        write.wait()


def local(members, queries, key_states, values, grad_out, segments):
    rows = queries.shape[1]
    reach = max(1, members // 2)
    any_space = pl.BlockSpec(memory_space=pl.ANY)
    low = jnp.bfloat16
    dma = pltpu.SemaphoreType.DMA
    pairs = H * rows * (reach + 1) * rows
    results = pl.pallas_call(
        functools.partial(kernel, members, reach),
        out_shape=(
            jax.ShapeDtypeStruct(queries.shape, low),
            jax.ShapeDtypeStruct(queries.shape, low),
            jax.ShapeDtypeStruct(key_states.shape, low),
            jax.ShapeDtypeStruct(values.shape, low),
        ),
        in_specs=[pl.BlockSpec(memory_space=pltpu.HBM)] * 5,
        out_specs=(any_space,) * 4,
        scratch_shapes=[
            pltpu.VMEM((KVH, rows, RATIO * HD), low),
            pltpu.VMEM((KVH, rows, RATIO * HD), low),
            pltpu.VMEM((reach + 1, KVH, 2, rows, HD), low),
            pltpu.VMEM((KVH, rows, RATIO * HD), low),
            pltpu.VMEM((KVH, rows, RATIO * HD), low),
            pltpu.VMEM((KVH, reach, 2, rows, HD), jnp.float32),
            pltpu.VMEM((reach, KVH, 2, rows, HD), low),
            pltpu.VMEM((reach, KVH, 2, rows, HD), low),
            pltpu.VMEM((KVH, 2, rows, HD), low),
            pltpu.VMEM((1, rows), jnp.int32),
            pltpu.VMEM((reach + 1, 8, rows), jnp.int32),
            pltpu.VMEM(((reach + 1) * rows, rows), jnp.float32),
            dma((4, KVH)),
            dma((4, KVH)),
            dma,
            dma((reach,)),
            dma((reach,)),
            dma((reach, KVH, 2)),
            dma((reach, KVH, 2)),
            dma((reach, KVH, 2)),
            dma((reach, KVH, 2)),
        ],
        compiler_params=pltpu.CompilerParams(
            collective_id=0, has_side_effects=True, vmem_limit_bytes=64 * 1024 * 1024
        ),
        cost_estimate=pl.CostEstimate(
            flops=12 * pairs * HD, bytes_accessed=4 * queries.size * 2 + 8 * values.size * 2, transcendentals=pairs
        ),
    )(queries, key_states, values, grad_out, segments)
    return pl.pallas_call(
        functools.partial(place, 2),
        out_shape=tuple(jax.ShapeDtypeStruct(result.shape, result.dtype) for result in results),
        in_specs=[pl.BlockSpec(memory_space=pltpu.HBM)] * 4,
        out_specs=(pl.BlockSpec(memory_space=pltpu.HBM),) * 4,
        scratch_shapes=[pltpu.VMEM(result.shape, result.dtype) for result in results]
        + [dma((4, 2)), dma((4, 2))],
        compiler_params=pltpu.CompilerParams(vmem_limit_bytes=64 * 1024 * 1024),
    )(*results)


def solution(mesh):
    spread = ("parts", "dp", "fsdp")
    wide = P(spread, "seq", None)
    return jax.shard_map(
        functools.partial(local, mesh.shape["seq"]),
        mesh=mesh,
        in_specs=(wide, wide, wide, wide, P(spread, "seq")),
        out_specs=(wide, wide, wide, wide),
        check_vma=False,
    )
```

```python
import functools

import jax
import jax.numpy as jnp
from jax import lax
from jax.experimental import pallas as pl
from jax.experimental.pallas import tpu as pltpu
from jax.sharding import PartitionSpec as P

H = 16
KVH = 4
HD = 128
RATIO = H // KVH
PAIR = 2
masked_bias = -1e30
MESH = pl.DeviceIdType.MESH


def kernel(
    members,
    reach,
    q_hbm,
    k_hbm,
    v_hbm,
    g_hbm,
    s_hbm,
    o_hbm,
    dq_hbm,
    dk_hbm,
    dv_hbm,
    q_buf,
    g_buf,
    kv_buf,
    o_buf,
    dq_buf,
    own,
    outgoing,
    incoming,
    dkv_buf,
    seg_row,
    seg_buf,
    bias,
    in_sem,
    out_sem,
    seg_sem,
    seg_send,
    seg_recv,
    kv_send,
    kv_recv,
    part_send,
    part_recv,
):
    me = lax.axis_index("seq")
    rows = q_buf.shape[1]
    keys = (reach + 1) * rows
    scale = HD**-0.5
    has_left = me > 0
    has_right = me < members - 1

    def columns(g, width):
        return pl.ds(pl.multiple_of(g * width, width), width)

    def kv_loads(g):
        return (
            pltpu.make_async_copy(k_hbm.at[0, :, columns(g, HD)], kv_buf.at[0, g, 0], in_sem.at[0, g]),
            pltpu.make_async_copy(v_hbm.at[0, :, columns(g, HD)], kv_buf.at[0, g, 1], in_sem.at[1, g]),
        )

    def loads(g):
        return (
            pltpu.make_async_copy(q_hbm.at[0, :, columns(g, RATIO * HD)], q_buf.at[g], in_sem.at[2, g]),
            pltpu.make_async_copy(g_hbm.at[0, :, columns(g, RATIO * HD)], g_buf.at[g], in_sem.at[3, g]),
        )

    def stores(g):
        return (
            pltpu.make_async_copy(o_buf.at[g], o_hbm.at[0, :, columns(g, RATIO * HD)], out_sem.at[0, g]),
            pltpu.make_async_copy(dq_buf.at[g], dq_hbm.at[0, :, columns(g, RATIO * HD)], out_sem.at[1, g]),
        )

    def kv_stores(g):
        return (
            pltpu.make_async_copy(dkv_buf.at[g, 0], dk_hbm.at[0, :, columns(g, HD)], out_sem.at[2, g]),
            pltpu.make_async_copy(dkv_buf.at[g, 1], dv_hbm.at[0, :, columns(g, HD)], out_sem.at[3, g]),
        )

    def kv_copy(w, g, t):
        return pltpu.make_async_remote_copy(
            src_ref=kv_buf.at[w, g],
            dst_ref=kv_buf.at[w + 1, g],
            send_sem=kv_send.at[w, g, t],
            recv_sem=kv_recv.at[w, g, t],
            device_id={"seq": lax.rem(me + 1, members)},
            device_id_type=MESH,
        )

    def seg_copy(w):
        return pltpu.make_async_remote_copy(
            src_ref=seg_buf.at[w],
            dst_ref=seg_buf.at[w + 1],
            send_sem=seg_send.at[w],
            recv_sem=seg_recv.at[w],
            device_id={"seq": lax.rem(me + 1, members)},
            device_id_type=MESH,
        )

    def part_copy(s, g, t):
        return pltpu.make_async_remote_copy(
            src_ref=outgoing.at[s, g, t],
            dst_ref=incoming.at[s, g, t],
            send_sem=part_send.at[s, g, t],
            recv_sem=part_recv.at[s, g, t],
            device_id={"seq": lax.rem(me + members - 1, members)},
            device_id_type=MESH,
        )

    seg_load = pltpu.make_async_copy(s_hbm, seg_row, seg_sem)
    seg_load.start()
    for g in range(KVH):
        for copy in kv_loads(g):
            copy.start()
    for g in range(KVH):
        for copy in loads(g):
            copy.start()

    barrier = pltpu.get_barrier_semaphore()

    @pl.when(has_left)
    def _():
        pl.semaphore_signal(
            barrier, inc=1, device_id={"seq": lax.rem(me + members - 1, members)}, device_id_type=MESH
        )

    @pl.when(has_right)
    def _():
        pl.semaphore_signal(
            barrier, inc=1, device_id={"seq": lax.rem(me + 1, members)}, device_id_type=MESH
        )

    for w in range(1, reach + 1):

        @pl.when(me < w)
        def _(w=w):
            kv_buf[w] = jnp.zeros(kv_buf.shape[1:], kv_buf.dtype)
            seg_buf[w] = jnp.zeros(seg_buf.shape[1:], seg_buf.dtype)

    seg_load.wait()
    seg_buf[0] = jnp.broadcast_to(seg_row[...], seg_buf.shape[1:])
    neighbours = has_left.astype(jnp.int32) + has_right.astype(jnp.int32)
    pl.semaphore_wait(barrier, neighbours)

    def send_own(g):
        for copy in kv_loads(g):
            copy.wait()

        @pl.when(has_right)
        def _():
            kv_copy(0, g, 0).start()

    def forward(g):
        for w in range(1, reach):

            @pl.when(me >= w)
            def _(w=w):
                for t in range(1):
                    kv_copy(w - 1, g, t).wait_recv()

                    @pl.when(has_right)
                    def _(t=t):
                        kv_copy(w, g, t).start()

    @pl.when(has_right)
    def _():
        seg_copy(0).start()

    send_own(0)
    send_own(1)
    forward(0)
    for w in range(1, reach + 1):

        @pl.when(me >= w)
        def _(w=w):
            seg_copy(w - 1).wait_recv()
            if w < reach:

                @pl.when(has_right)
                def _():
                    seg_copy(w).start()

    row_ids = lax.broadcasted_iota(jnp.int32, (rows, rows), 0)
    column_ids = lax.broadcasted_iota(jnp.int32, (rows, rows), 1)
    own_document = jnp.broadcast_to(seg_buf[0, 0:1].astype(jnp.float32), (rows, rows))
    for w in range(reach + 1):
        key_document = jnp.broadcast_to(seg_buf[w, 0:1].astype(jnp.float32), (rows, rows)).T
        allowed = key_document == own_document
        if w == 0:
            allowed = jnp.logical_and(allowed, row_ids <= column_ids)
        block = jnp.where(allowed, 0.0, masked_bias)
        bias[pl.ds(w * rows, rows)] = jnp.where(me >= w, block, masked_bias)

    def contract(left, right):
        return lax.dot_general(left, right, (((1,), (1,)), ((), ())), preferred_element_type=jnp.float32)

    def product(left, right):
        return jnp.dot(left, right, preferred_element_type=jnp.float32)

    def compute(g):
        key = kv_buf[:, g, 0].reshape(keys, HD)
        value = kv_buf[:, g, 1].reshape(keys, HD)
        key_t = key.T
        value_t = value.T
        shift = jnp.concatenate([bias[...]] * PAIR, axis=1)
        key_sum = value_sum = None
        for first in range(0, RATIO, PAIR):
            heads = range(first, first + PAIR)
            query = jnp.concatenate([q_buf[g, :, h * HD : (h + 1) * HD] for h in heads], axis=0)
            grad = jnp.concatenate([g_buf[g, :, h * HD : (h + 1) * HD] for h in heads], axis=0)
            scores = contract(key, query) * scale + shift
            top = jnp.max(scores, axis=0, keepdims=True)
            exponents = jnp.exp(scores - top)
            weights = exponents * (1.0 / jnp.sum(exponents, axis=0, keepdims=True))
            weights_low = weights.astype(jnp.bfloat16)
            spread = contract(value, grad)
            delta = jnp.sum(weights_low.astype(jnp.float32) * spread, axis=0, keepdims=True)
            score_grad = (weights * (spread - delta)).astype(jnp.bfloat16)
            attended = product(value_t, weights_low).T.astype(jnp.bfloat16)
            query_grad = (product(key_t, score_grad) * scale).T.astype(jnp.bfloat16)
            for at, h in enumerate(heads):
                o_buf[g, :, h * HD : (h + 1) * HD] = attended[at * rows : (at + 1) * rows]
                dq_buf[g, :, h * HD : (h + 1) * HD] = query_grad[at * rows : (at + 1) * rows]
            key_part = product(score_grad, query)
            value_part = product(weights_low, grad)
            key_sum = key_part if key_sum is None else key_sum + key_part
            value_sum = value_part if value_sum is None else value_sum + value_part
        key_sum = key_sum * scale
        for w in range(reach + 1):
            block = slice(w * rows, (w + 1) * rows)
            if w < reach:
                own[g, w, 0] = key_sum[block]
                own[g, w, 1] = value_sum[block]
            else:
                outgoing[w - 1, g, 0] = key_sum[block].astype(jnp.bfloat16)
                outgoing[w - 1, g, 1] = value_sum[block].astype(jnp.bfloat16)

    def pass_on(g):
        for w in range(reach - 1, 0, -1):

            @pl.when(me >= w)
            def _(w=w):
                for t in (1, 0):

                    @pl.when(has_right)
                    def _(t=t):
                        part_copy(w, g, t).wait_recv()
                        total = own[g, w, t] + incoming[w, g, t].astype(jnp.float32)
                        outgoing[w - 1, g, t] = total.astype(jnp.bfloat16)

                    @pl.when(jnp.logical_not(has_right))
                    def _(t=t):
                        outgoing[w - 1, g, t] = own[g, w, t].astype(jnp.bfloat16)

                    part_copy(w - 1, g, t).start()

    def finish(g):
        @pl.when(has_right)
        def _():
            part_copy(0, g, 1).wait_recv()
            part_copy(0, g, 0).wait_recv()
            dkv_buf[g] = (own[g, 0] + incoming[0, g].astype(jnp.float32)).astype(jnp.bfloat16)

        @pl.when(jnp.logical_not(has_right))
        def _():
            dkv_buf[g] = own[g, 0].astype(jnp.bfloat16)

        for copy in kv_stores(g):
            copy.start()

    def step(g, carry):
        @pl.when(g + 2 < KVH)
        def _():
            send_own(g + 2)

        @pl.when(g + 1 < KVH)
        def _():
            forward(g + 1)

        @pl.when(me >= reach)
        def _():
            kv_copy(reach - 1, g, 0).wait_recv()

        for copy in loads(g):
            copy.wait()
        compute(g)

        @pl.when(me >= reach)
        def _():
            part_copy(reach - 1, g, 1).start()
            part_copy(reach - 1, g, 0).start()

        for copy in stores(g):
            copy.start()

        @pl.when(g >= 2)
        def _():
            pass_on(g - 2)

        return carry

    lax.fori_loop(0, KVH, step, 0)
    pass_on(KVH - 2)
    pass_on(KVH - 1)
    for g in range(KVH):
        finish(g)

    for w in range(reach):

        @pl.when(jnp.logical_and(has_right, me >= w))
        def _(w=w):
            seg_copy(w).wait_send()
            for g in range(KVH):
                kv_copy(w, g, 0).wait_send()

        @pl.when(me >= w + 1)
        def _(w=w):
            for g in range(KVH):
                part_copy(w, g, 0).wait_send()
                part_copy(w, g, 1).wait_send()

    for g in range(KVH):
        for copy in stores(g) + kv_stores(g):
            copy.wait()


def place(parts, *refs):
    sources, results, held, read_sem, write_sem = refs[0:4], refs[4:8], refs[8:12], refs[12], refs[13]
    pairs = []
    for i in range(4):
        size = sources[i].shape[1] // parts
        for j in range(parts):
            at = (slice(None), pl.ds(j * size, size))
            pairs.append(
                (
                    pltpu.make_async_copy(sources[i].at[at], held[i].at[at], read_sem.at[i, j]),
                    pltpu.make_async_copy(held[i].at[at], results[i].at[at], write_sem.at[i, j]),
                )
            )
    for read, _ in pairs:
        read.start()
    for read, write in pairs:
        read.wait()
        write.start()
    for _, write in pairs:
        write.wait()


def local(members, queries, key_states, values, grad_out, segments):
    rows = queries.shape[1]
    reach = max(1, members // 2)
    any_space = pl.BlockSpec(memory_space=pl.ANY)
    low = jnp.bfloat16
    dma = pltpu.SemaphoreType.DMA
    pairs = H * rows * (reach + 1) * rows
    results = pl.pallas_call(
        functools.partial(kernel, members, reach),
        out_shape=(
            jax.ShapeDtypeStruct(queries.shape, low),
            jax.ShapeDtypeStruct(queries.shape, low),
            jax.ShapeDtypeStruct(key_states.shape, low),
            jax.ShapeDtypeStruct(values.shape, low),
        ),
        in_specs=[pl.BlockSpec(memory_space=pltpu.HBM)] * 5,
        out_specs=(any_space,) * 4,
        scratch_shapes=[
            pltpu.VMEM((KVH, rows, RATIO * HD), low),
            pltpu.VMEM((KVH, rows, RATIO * HD), low),
            pltpu.VMEM((reach + 1, KVH, 2, rows, HD), low),
            pltpu.VMEM((KVH, rows, RATIO * HD), low),
            pltpu.VMEM((KVH, rows, RATIO * HD), low),
            pltpu.VMEM((KVH, reach, 2, rows, HD), jnp.float32),
            pltpu.VMEM((reach, KVH, 2, rows, HD), low),
            pltpu.VMEM((reach, KVH, 2, rows, HD), low),
            pltpu.VMEM((KVH, 2, rows, HD), low),
            pltpu.VMEM((1, rows), jnp.int32),
            pltpu.VMEM((reach + 1, 8, rows), jnp.int32),
            pltpu.VMEM(((reach + 1) * rows, rows), jnp.float32),
            dma((4, KVH)),
            dma((4, KVH)),
            dma,
            dma((reach,)),
            dma((reach,)),
            dma((reach, KVH, 2)),
            dma((reach, KVH, 2)),
            dma((reach, KVH, 2)),
            dma((reach, KVH, 2)),
        ],
        compiler_params=pltpu.CompilerParams(
            collective_id=0, has_side_effects=True, vmem_limit_bytes=64 * 1024 * 1024
        ),
        cost_estimate=pl.CostEstimate(
            flops=12 * pairs * HD, bytes_accessed=4 * queries.size * 2 + 8 * values.size * 2, transcendentals=pairs
        ),
    )(queries, key_states, values, grad_out, segments)
    return pl.pallas_call(
        functools.partial(place, 2),
        out_shape=tuple(jax.ShapeDtypeStruct(result.shape, result.dtype) for result in results),
        in_specs=[pl.BlockSpec(memory_space=pltpu.HBM)] * 4,
        out_specs=(pl.BlockSpec(memory_space=pltpu.HBM),) * 4,
        scratch_shapes=[pltpu.VMEM(result.shape, result.dtype) for result in results]
        + [dma((4, 2)), dma((4, 2))],
        compiler_params=pltpu.CompilerParams(vmem_limit_bytes=64 * 1024 * 1024),
    )(*results)


def solution(mesh):
    spread = ("parts", "dp", "fsdp")
    wide = P(spread, "seq", None)
    return jax.shard_map(
        functools.partial(local, mesh.shape["seq"]),
        mesh=mesh,
        in_specs=(wide, wide, wide, wide, P(spread, "seq")),
        out_specs=(wide, wide, wide, wide),
        check_vma=False,
    )
```

```python
import functools

import jax
import jax.numpy as jnp
from jax import lax
from jax.experimental import pallas as pl
from jax.experimental.pallas import tpu as pltpu
from jax.sharding import PartitionSpec as P

H = 16
KVH = 4
HD = 128
RATIO = H // KVH
PAIR = 2
masked_bias = -1e30
MESH = pl.DeviceIdType.MESH


def kernel(
    members,
    reach,
    q_hbm,
    k_hbm,
    v_hbm,
    g_hbm,
    s_hbm,
    o_hbm,
    dq_hbm,
    dk_hbm,
    dv_hbm,
    q_buf,
    g_buf,
    kv_buf,
    o_buf,
    dq_buf,
    own,
    outgoing,
    incoming,
    dkv_buf,
    seg_row,
    seg_buf,
    bias,
    in_sem,
    out_sem,
    seg_sem,
    seg_send,
    seg_recv,
    kv_send,
    kv_recv,
    part_send,
    part_recv,
):
    me = lax.axis_index("seq")
    rows = q_buf.shape[1]
    keys = (reach + 1) * rows
    scale = HD**-0.5
    has_left = me > 0
    has_right = me < members - 1

    def columns(g, width):
        return pl.ds(pl.multiple_of(g * width, width), width)

    def kv_loads(g):
        return (
            pltpu.make_async_copy(k_hbm.at[0, :, columns(g, HD)], kv_buf.at[0, g, 0], in_sem.at[0, g]),
            pltpu.make_async_copy(v_hbm.at[0, :, columns(g, HD)], kv_buf.at[0, g, 1], in_sem.at[1, g]),
        )

    def loads(g):
        return (
            pltpu.make_async_copy(q_hbm.at[0, :, columns(g, RATIO * HD)], q_buf.at[g], in_sem.at[2, g]),
            pltpu.make_async_copy(g_hbm.at[0, :, columns(g, RATIO * HD)], g_buf.at[g], in_sem.at[3, g]),
        )

    def stores(g):
        return (
            pltpu.make_async_copy(o_buf.at[g], o_hbm.at[0, :, columns(g, RATIO * HD)], out_sem.at[0, g]),
            pltpu.make_async_copy(dq_buf.at[g], dq_hbm.at[0, :, columns(g, RATIO * HD)], out_sem.at[1, g]),
        )

    def kv_stores(g):
        return (
            pltpu.make_async_copy(dkv_buf.at[g, 0], dk_hbm.at[0, :, columns(g, HD)], out_sem.at[2, g]),
            pltpu.make_async_copy(dkv_buf.at[g, 1], dv_hbm.at[0, :, columns(g, HD)], out_sem.at[3, g]),
        )

    def kv_copy(w, g, t):
        return pltpu.make_async_remote_copy(
            src_ref=kv_buf.at[w, g],
            dst_ref=kv_buf.at[w + 1, g],
            send_sem=kv_send.at[w, g, t],
            recv_sem=kv_recv.at[w, g, t],
            device_id={"seq": lax.rem(me + 1, members)},
            device_id_type=MESH,
        )

    def seg_copy(w):
        return pltpu.make_async_remote_copy(
            src_ref=seg_buf.at[w],
            dst_ref=seg_buf.at[w + 1],
            send_sem=seg_send.at[w],
            recv_sem=seg_recv.at[w],
            device_id={"seq": lax.rem(me + 1, members)},
            device_id_type=MESH,
        )

    def part_copy(s, g, t):
        return pltpu.make_async_remote_copy(
            src_ref=outgoing.at[s, g, t],
            dst_ref=incoming.at[s, g, t],
            send_sem=part_send.at[s, g, t],
            recv_sem=part_recv.at[s, g, t],
            device_id={"seq": lax.rem(me + members - 1, members)},
            device_id_type=MESH,
        )

    seg_load = pltpu.make_async_copy(s_hbm, seg_row, seg_sem)
    seg_load.start()
    for g in range(KVH):
        for copy in kv_loads(g):
            copy.start()
    for g in range(KVH):
        for copy in loads(g):
            copy.start()

    barrier = pltpu.get_barrier_semaphore()

    @pl.when(has_left)
    def _():
        pl.semaphore_signal(
            barrier, inc=1, device_id={"seq": lax.rem(me + members - 1, members)}, device_id_type=MESH
        )

    @pl.when(has_right)
    def _():
        pl.semaphore_signal(
            barrier, inc=1, device_id={"seq": lax.rem(me + 1, members)}, device_id_type=MESH
        )

    for w in range(1, reach + 1):

        @pl.when(me < w)
        def _(w=w):
            kv_buf[w] = jnp.zeros(kv_buf.shape[1:], kv_buf.dtype)
            seg_buf[w] = jnp.zeros(seg_buf.shape[1:], seg_buf.dtype)

    seg_load.wait()
    seg_buf[0] = jnp.broadcast_to(seg_row[...], seg_buf.shape[1:])
    neighbours = has_left.astype(jnp.int32) + has_right.astype(jnp.int32)
    pl.semaphore_wait(barrier, neighbours)

    def send_own(g):
        for copy in kv_loads(g):
            copy.wait()

        @pl.when(has_right)
        def _():
            kv_copy(0, g, 0).start()

    def forward(g):
        for w in range(1, reach):

            @pl.when(me >= w)
            def _(w=w):
                for t in range(1):
                    kv_copy(w - 1, g, t).wait_recv()

                    @pl.when(has_right)
                    def _(t=t):
                        kv_copy(w, g, t).start()

    @pl.when(has_right)
    def _():
        seg_copy(0).start()

    send_own(0)
    forward(0)
    send_own(1)
    for w in range(1, reach + 1):

        @pl.when(me >= w)
        def _(w=w):
            seg_copy(w - 1).wait_recv()
            if w < reach:

                @pl.when(has_right)
                def _():
                    seg_copy(w).start()

    row_ids = lax.broadcasted_iota(jnp.int32, (rows, rows), 0)
    column_ids = lax.broadcasted_iota(jnp.int32, (rows, rows), 1)
    own_document = jnp.broadcast_to(seg_buf[0, 0:1].astype(jnp.float32), (rows, rows))
    for w in range(reach + 1):
        key_document = jnp.broadcast_to(seg_buf[w, 0:1].astype(jnp.float32), (rows, rows)).T
        allowed = key_document == own_document
        if w == 0:
            allowed = jnp.logical_and(allowed, row_ids <= column_ids)
        block = jnp.where(allowed, 0.0, masked_bias)
        bias[pl.ds(w * rows, rows)] = jnp.where(me >= w, block, masked_bias)

    def contract(left, right):
        return lax.dot_general(left, right, (((1,), (1,)), ((), ())), preferred_element_type=jnp.float32)

    def product(left, right):
        return jnp.dot(left, right, preferred_element_type=jnp.float32)

    def compute(g):
        key = kv_buf[:, g, 0].reshape(keys, HD)
        value = kv_buf[:, g, 1].reshape(keys, HD)
        key_t = key.T
        value_t = value.T
        shift = jnp.concatenate([bias[...]] * PAIR, axis=1)
        key_sum = value_sum = None
        for first in range(0, RATIO, PAIR):
            heads = range(first, first + PAIR)
            query = jnp.concatenate([q_buf[g, :, h * HD : (h + 1) * HD] for h in heads], axis=0)
            grad = jnp.concatenate([g_buf[g, :, h * HD : (h + 1) * HD] for h in heads], axis=0)
            scores = contract(key, query) * scale + shift
            top = jnp.max(scores, axis=0, keepdims=True)
            exponents = jnp.exp(scores - top)
            weights = exponents * (1.0 / jnp.sum(exponents, axis=0, keepdims=True))
            weights_low = weights.astype(jnp.bfloat16)
            spread = contract(value, grad)
            delta = jnp.sum(weights_low.astype(jnp.float32) * spread, axis=0, keepdims=True)
            score_grad = (weights * (spread - delta)).astype(jnp.bfloat16)
            attended = product(value_t, weights_low).T.astype(jnp.bfloat16)
            query_grad = (product(key_t, score_grad) * scale).T.astype(jnp.bfloat16)
            for at, h in enumerate(heads):
                o_buf[g, :, h * HD : (h + 1) * HD] = attended[at * rows : (at + 1) * rows]
                dq_buf[g, :, h * HD : (h + 1) * HD] = query_grad[at * rows : (at + 1) * rows]
            key_part = product(score_grad, query)
            value_part = product(weights_low, grad)
            key_sum = key_part if key_sum is None else key_sum + key_part
            value_sum = value_part if value_sum is None else value_sum + value_part
        key_sum = key_sum * scale
        for w in range(reach + 1):
            block = slice(w * rows, (w + 1) * rows)
            if w < reach:
                own[g, w, 0] = key_sum[block]
                own[g, w, 1] = value_sum[block]
            else:
                outgoing[w - 1, g, 0] = key_sum[block].astype(jnp.bfloat16)
                outgoing[w - 1, g, 1] = value_sum[block].astype(jnp.bfloat16)

    def pass_on(g):
        for w in range(reach - 1, 0, -1):

            @pl.when(me >= w)
            def _(w=w):
                for t in (1, 0):

                    @pl.when(has_right)
                    def _(t=t):
                        part_copy(w, g, t).wait_recv()
                        total = own[g, w, t] + incoming[w, g, t].astype(jnp.float32)
                        outgoing[w - 1, g, t] = total.astype(jnp.bfloat16)

                    @pl.when(jnp.logical_not(has_right))
                    def _(t=t):
                        outgoing[w - 1, g, t] = own[g, w, t].astype(jnp.bfloat16)

                    part_copy(w - 1, g, t).start()

    def finish(g):
        @pl.when(has_right)
        def _():
            part_copy(0, g, 1).wait_recv()
            part_copy(0, g, 0).wait_recv()
            dkv_buf[g] = (own[g, 0] + incoming[0, g].astype(jnp.float32)).astype(jnp.bfloat16)

        @pl.when(jnp.logical_not(has_right))
        def _():
            dkv_buf[g] = own[g, 0].astype(jnp.bfloat16)

        for copy in kv_stores(g):
            copy.start()

    def step(g, carry):
        @pl.when(g + 2 < KVH)
        def _():
            send_own(g + 2)

        @pl.when(g + 1 < KVH)
        def _():
            forward(g + 1)

        @pl.when(me >= reach)
        def _():
            kv_copy(reach - 1, g, 0).wait_recv()

        for copy in loads(g):
            copy.wait()
        compute(g)

        @pl.when(me >= reach)
        def _():
            part_copy(reach - 1, g, 1).start()
            part_copy(reach - 1, g, 0).start()

        for copy in stores(g):
            copy.start()

        @pl.when(g >= 2)
        def _():
            pass_on(g - 2)

        return carry

    lax.fori_loop(0, KVH, step, 0)
    pass_on(KVH - 2)
    pass_on(KVH - 1)
    for g in range(KVH):
        finish(g)

    for w in range(reach):

        @pl.when(jnp.logical_and(has_right, me >= w))
        def _(w=w):
            seg_copy(w).wait_send()
            for g in range(KVH):
                kv_copy(w, g, 0).wait_send()

        @pl.when(me >= w + 1)
        def _(w=w):
            for g in range(KVH):
                part_copy(w, g, 0).wait_send()
                part_copy(w, g, 1).wait_send()

    for g in range(KVH):
        for copy in stores(g) + kv_stores(g):
            copy.wait()


def place(parts, *refs):
    sources, results, held, read_sem, write_sem = refs[0:4], refs[4:8], refs[8:12], refs[12], refs[13]
    pairs = []
    for i in range(4):
        size = sources[i].shape[1] // parts
        for j in range(parts):
            at = (slice(None), pl.ds(j * size, size))
            pairs.append(
                (
                    pltpu.make_async_copy(sources[i].at[at], held[i].at[at], read_sem.at[i, j]),
                    pltpu.make_async_copy(held[i].at[at], results[i].at[at], write_sem.at[i, j]),
                )
            )
    for read, _ in pairs:
        read.start()
    for read, write in pairs:
        read.wait()
        write.start()
    for _, write in pairs:
        write.wait()


def local(members, queries, key_states, values, grad_out, segments):
    rows = queries.shape[1]
    reach = max(1, members // 2)
    any_space = pl.BlockSpec(memory_space=pl.ANY)
    low = jnp.bfloat16
    dma = pltpu.SemaphoreType.DMA
    pairs = H * rows * (reach + 1) * rows
    results = pl.pallas_call(
        functools.partial(kernel, members, reach),
        out_shape=(
            jax.ShapeDtypeStruct(queries.shape, low),
            jax.ShapeDtypeStruct(queries.shape, low),
            jax.ShapeDtypeStruct(key_states.shape, low),
            jax.ShapeDtypeStruct(values.shape, low),
        ),
        in_specs=[pl.BlockSpec(memory_space=pltpu.HBM)] * 5,
        out_specs=(any_space,) * 4,
        scratch_shapes=[
            pltpu.VMEM((KVH, rows, RATIO * HD), low),
            pltpu.VMEM((KVH, rows, RATIO * HD), low),
            pltpu.VMEM((reach + 1, KVH, 2, rows, HD), low),
            pltpu.VMEM((KVH, rows, RATIO * HD), low),
            pltpu.VMEM((KVH, rows, RATIO * HD), low),
            pltpu.VMEM((KVH, reach, 2, rows, HD), jnp.float32),
            pltpu.VMEM((reach, KVH, 2, rows, HD), low),
            pltpu.VMEM((reach, KVH, 2, rows, HD), low),
            pltpu.VMEM((KVH, 2, rows, HD), low),
            pltpu.VMEM((1, rows), jnp.int32),
            pltpu.VMEM((reach + 1, 8, rows), jnp.int32),
            pltpu.VMEM(((reach + 1) * rows, rows), jnp.float32),
            dma((4, KVH)),
            dma((4, KVH)),
            dma,
            dma((reach,)),
            dma((reach,)),
            dma((reach, KVH, 2)),
            dma((reach, KVH, 2)),
            dma((reach, KVH, 2)),
            dma((reach, KVH, 2)),
        ],
        compiler_params=pltpu.CompilerParams(
            collective_id=0, has_side_effects=True, vmem_limit_bytes=64 * 1024 * 1024
        ),
        cost_estimate=pl.CostEstimate(
            flops=12 * pairs * HD, bytes_accessed=4 * queries.size * 2 + 8 * values.size * 2, transcendentals=pairs
        ),
    )(queries, key_states, values, grad_out, segments)
    return pl.pallas_call(
        functools.partial(place, 2),
        out_shape=tuple(jax.ShapeDtypeStruct(result.shape, result.dtype) for result in results),
        in_specs=[pl.BlockSpec(memory_space=pltpu.HBM)] * 4,
        out_specs=(pl.BlockSpec(memory_space=pltpu.HBM),) * 4,
        scratch_shapes=[pltpu.VMEM(result.shape, result.dtype) for result in results]
        + [dma((4, 2)), dma((4, 2))],
        compiler_params=pltpu.CompilerParams(vmem_limit_bytes=64 * 1024 * 1024),
    )(*results)


def solution(mesh):
    spread = ("parts", "dp", "fsdp")
    wide = P(spread, "seq", None)
    return jax.shard_map(
        functools.partial(local, mesh.shape["seq"]),
        mesh=mesh,
        in_specs=(wide, wide, wide, wide, P(spread, "seq")),
        out_specs=(wide, wide, wide, wide),
        check_vma=False,
    )
```
